512 devices in a mesh: row: 16 (over y_lo, x, core), col: 32 (over z, y_hi).
Axes of the slice: x: 4, y: 8 (y_hi: 4, y_lo: 2; y = y_hi * 2 + y_lo), z: 8, core: 2. Of those that a mesh axis runs over, the one named last changes fastest.
Arguments:
- query_tokens: bfloat16 [512, 192, 1024], P('row', 'col'), may hold values from -11 to 11
- key_tokens: bfloat16 [512, 192, 1024], P('row', 'col'), may hold values from -6 to 6
- value_tokens: bfloat16 [512, 192, 1024], P('row', 'col'), may hold values from -6 to 6
- merge_sizes: int32 [512, 192], P('row', 'col'), may hold values from 1 to 16
- w_out: bfloat16 [1024, 1024], P(None, 'row'), may hold values from -0.1875 to 0.1875
Outputs:
- mixed: bfloat16 [512, 192, 1024], P('row', 'col')
The draws below stay inside these ranges and needn't reach their ends.
All inputs are finite; a program needn't handle non-finite values.
Results may differ from the reference program's by a relative error of at most 0.0085.
Values may be sent and summed in bfloat16 or wider, within the bound.
No kernel may reach another device: no remote copies, remote signals or barrier semaphores. Data moves between devices by JAX's collectives and lax.ppermute only.
A program may use at most 64 MiB of HBM per device.

```python
import jax
import jax.numpy as jnp
from jax import lax

HEADS = 16
HEAD = 64
D = 1024
GR = 512
GC = 192


def draw_query_tokens(key, part):
    key = jax.random.fold_in(key, 11)
    shape_full = (GR, GC, HEADS, HEAD)
    background = jax.random.truncated_normal(key, -6.0, 6.0, shape_full, jnp.float32)
    return background.reshape(GR, GC, HEADS * HEAD).astype(jnp.bfloat16)


def draw_key_tokens(key, part):
    key = jax.random.fold_in(key, 23)
    shape_full = (GR, GC, HEADS, HEAD)
    background = jax.random.truncated_normal(key, -6.0, 6.0, shape_full, jnp.float32)
    return background.reshape(GR, GC, HEADS * HEAD).astype(jnp.bfloat16)


def set_ends(entries, own_key, low, largest):
    longest = entries.shape.index(max(entries.shape))
    spots = []
    for shift in (0, 1):
        where = [jax.random.randint(jax.random.fold_in(own_key, axis), (), 0, length) for axis, length in enumerate(entries.shape)]
        where[longest] = (where[longest] + shift) % entries.shape[longest]
        spots.append(tuple(where))
    return entries.at[spots[0]].set(low).at[spots[1]].set(largest)


def level_of(rng, shape, shards, least, largest):
    level = 1.0
    for dim, shards_of in shards:
        steps = jax.random.uniform(jax.random.fold_in(jax.random.fold_in(rng, 6), dim), (shards_of,), jnp.float32, least / len(shards), largest / len(shards))
        level = level * jnp.repeat(jnp.exp(steps), shape[dim] // shards_of).reshape((-1,) + (1,) * (len(shape) - 1 - dim))
    return level


def centred(key, dims, deviation, most, shards=(), kind=jnp.bfloat16):
    drawn = deviation * jax.random.normal(key, dims, jnp.float32)
    if shards:
        drawn = drawn * level_of(key, dims, shards, -0.22, 0.18)
    return jnp.clip(drawn, -most, most).astype(kind)


def setup_inputs(seed: int = 0) -> dict:
    splits = jax.random.split(jax.random.key(seed), 6)
    return {
        "query_tokens": draw_query_tokens(jax.random.fold_in(splits[5], 71), 0),
        "key_tokens": draw_key_tokens(jax.random.fold_in(splits[5], 71), 0),
        "value_tokens": centred(splits[2], (GR, GC, D), 1.0, 6.0, ((0, 16), (1, 32))),
        "merge_sizes": set_ends(jax.random.randint(splits[3], (GR, GC), 1, 17), jax.random.fold_in(splits[3], 1), 1, 16).astype(jnp.int32),
        "w_out": centred(splits[4], (D, D), D ** -0.5, 0.1875, ((1, 16),)),
    }


def attend_line(queries, keys_line, values_line, bias_line):
    scores = jnp.einsum("rhd,khd->hrk", queries.astype(jnp.float32), keys_line.astype(jnp.float32)) * (HEAD ** -0.5)
    scores = scores + bias_line.astype(jnp.float32)[None, None, :]
    highest = jnp.max(scores, axis=-1, keepdims=True)
    weights = jnp.exp(scores - highest)
    summed = jnp.sum(weights, axis=-1)
    rounded = lax.optimization_barrier(weights.astype(jnp.bfloat16))
    combined = jnp.einsum("hrk,khd->rhd", rounded.astype(jnp.float32), values_line.astype(jnp.float32))
    return (combined / jnp.transpose(summed)[:, :, None]).astype(jnp.bfloat16)


def run_line(operands):
    return attend_line(operands[0], operands[1], operands[2], operands[3])


def reference(query_tokens, key_tokens, value_tokens, merge_sizes, w_out):
    half_width = (HEADS // 2) * HEAD
    key_bias = lax.optimization_barrier(jnp.log(merge_sizes.astype(jnp.float32)).astype(jnp.bfloat16))

    def heads_of(source, head_group):
        return source[:, :, head_group * half_width:(head_group + 1) * half_width].reshape(GR, GC, HEADS // 2, HEAD)

    column_parts = tuple(jnp.swapaxes(heads_of(source, 0), 0, 1) for source in (query_tokens, key_tokens, value_tokens))
    column_out = lax.map(run_line, column_parts + (jnp.transpose(key_bias),))
    column_out = jnp.swapaxes(column_out, 0, 1).reshape(GR, GC, half_width)
    row_parts = tuple(heads_of(source, 1) for source in (query_tokens, key_tokens, value_tokens))
    row_out = lax.map(run_line, row_parts + (key_bias,)).reshape(GR, GC, half_width)
    joined = jnp.concatenate([column_out, row_out], axis=-1).reshape(GR * GC, HEADS * HEAD)
    result = jnp.dot(joined, w_out, preferred_element_type=jnp.float32).astype(jnp.bfloat16)
    return result.reshape(GR, GC, HEADS * HEAD)
```

```python
import jax
import jax.numpy as jnp
from jax import lax
from jax.experimental import pallas as pl
from jax.experimental.pallas import tpu as pltpu
from jax.sharding import PartitionSpec as P

HEADS = 16
HEAD = 64
HALF = HEADS // 2
WIDTH = HALF * HEAD
LOG2E = 1.4426950408889634
VMEM_LIMIT = 48 * 1024 * 1024


def swap_halves(tile):
    return pltpu.roll(tile, HEAD, tile.ndim - 1)


def low_lanes(shape):
    return lax.broadcasted_iota(jnp.int32, shape, len(shape) - 1) < HEAD


def bias_lanes(merges, first_token, first_lane, count):
    tokens, rows = merges.shape
    bias = jnp.log(merges.astype(jnp.float32)).astype(jnp.bfloat16).astype(jnp.float32)
    token = lax.broadcasted_iota(jnp.int32, (tokens, 128), 0) - first_token
    lane = lax.broadcasted_iota(jnp.int32, (tokens, 128), 1) - first_lane
    pick = ((token == lane) & (lane >= 0) & (lane < count)).astype(jnp.float32)
    return lax.dot_general(
        bias.astype(jnp.bfloat16),
        pick.astype(jnp.bfloat16),
        (((0,), (0,)), ((), ())),
        preferred_element_type=jnp.float32,
    )


def pack_rows_kernel(q_ref, k_ref, v_ref, m_ref, out_ref):
    bias = bias_lanes(m_ref[...], 0, 0, 6)
    low = low_lanes((6, 32, 128))
    for pair in range(HALF // 2):
        lanes = slice(128 * pair, 128 * pair + 128)
        q = q_ref[:, :, lanes].astype(jnp.float32)
        k = k_ref[:, :, lanes].astype(jnp.float32)
        v = v_ref[:, :, lanes].astype(jnp.float32)
        sq, sk, sv = swap_halves(q), swap_halves(k), swap_halves(v)
        for odd in range(2):
            qk = jnp.where(low, sq, k) if odd else jnp.where(low, q, sk)
            vv = (
                jnp.where(low[:3], sv[:3], v[3:])
                if odd
                else jnp.where(low[:3], v[:3], sv[3:])
            )
            for rg in range(4):
                rows = slice(8 * rg, 8 * rg + 8)
                block = rg * 8 + 2 * pair + odd
                out_ref[block, 0:6] = qk[:, rows].astype(jnp.bfloat16)
                out_ref[block, 6:9] = vv[:, rows].astype(jnp.bfloat16)
                out_ref[block, 9] = bias[rows].astype(jnp.bfloat16)


def pack_columns_kernel(q_ref, k_ref, v_ref, m_ref, out_ref):
    low = low_lanes((6, 32, 128))
    biases = [bias_lanes(m_ref[...], 3 * g, HEAD, 3) for g in range(2)]
    for pair in range(HALF // 2):
        lanes = slice(128 * pair, 128 * pair + 128)
        q = q_ref[:, :, lanes].astype(jnp.float32)
        k = k_ref[:, :, lanes].astype(jnp.float32)
        v = v_ref[:, :, lanes].astype(jnp.float32)
        sq, sk, sv = swap_halves(q), swap_halves(k), swap_halves(v)
        for odd in range(2):
            qk = jnp.where(low, sq, k) if odd else jnp.where(low, q, sk)
            to_low, to_high = (sv, v) if odd else (v, sv)
            for g in range(2):
                block = 2 * (2 * pair + odd) + g
                out_ref[block, 0:3] = qk[3 * g : 3 * g + 3].astype(jnp.bfloat16)
                out_ref[block, 3] = jnp.where(
                    low[0], to_low[3 * g], to_high[3 * g + 1]
                ).astype(jnp.bfloat16)
                out_ref[block, 4] = jnp.where(
                    low[0], to_low[3 * g + 2], biases[g]
                ).astype(jnp.bfloat16)


def attend(q, k, v, bias):
    scores = lax.dot_general(
        k, q, (((1,), (1,)), ((), ())), preferred_element_type=jnp.float32
    )
    scores = scores * (HEAD**-0.5 * LOG2E) + bias * LOG2E
    weights = jnp.exp2(scores - jnp.max(scores, axis=0, keepdims=True))
    totals = jnp.sum(weights, axis=0, keepdims=True)
    summed = lax.dot_general(
        v,
        weights.astype(jnp.bfloat16),
        (((0,), (0,)), ((), ())),
        preferred_element_type=jnp.float32,
    )
    return summed / totals


def attend_rows_kernel(in_ref, out_ref, qk_ref, v_ref, b_ref, o_ref):
    for t in range(6):
        qk_ref[t * 256 : t * 256 + 256] = (
            in_ref[:, t].astype(jnp.float32).reshape(256, 128)
        )
    for j in range(3):
        v_ref[j * 256 : j * 256 + 256] = (
            in_ref[:, 6 + j].astype(jnp.float32).reshape(256, 128)
        )
    b_ref[...] = in_ref[:, 9].astype(jnp.float32).reshape(256, 128)
    for r in range(8):
        qk = qk_ref[pl.ds(r, 192, stride=8), :].astype(jnp.bfloat16)
        vv = v_ref[pl.ds(r, 96, stride=8), :].astype(jnp.bfloat16)
        bb = b_ref[pl.ds(r, 32, stride=8), :]
        v = jnp.concatenate([vv[:, :HEAD], vv[:, HEAD:]], axis=0)
        bias = jnp.concatenate([bb[:, t : t + 1] for t in range(6)], axis=0)
        out = attend(qk[:, :HEAD], qk[:, HEAD:], v, bias)
        out = out.T
        o_ref[pl.ds(r, 96, stride=8), :] = jnp.concatenate([out[:96], out[96:]], axis=1)
    for j in range(3):
        out_ref[:, j] = (
            o_ref[j * 256 : j * 256 + 256].reshape(32, 8, 128).astype(jnp.bfloat16)
        )


def attend_columns_kernel(in_ref, out_ref):
    tail = in_ref[:, 4].reshape(512, 128)
    vv = in_ref[:, 3].reshape(512, 128)
    values = (vv[:, :HEAD], vv[:, HEAD:], tail[:, :HEAD])
    outs = []
    for j in range(3):
        qk = in_ref[:, j].reshape(512, 128)
        bias = tail[:, HEAD + j : HEAD + j + 1].astype(jnp.float32)
        pieces = [
            attend(qk[start : start + 256, :HEAD], qk[:, HEAD:], values[j], bias)
            for start in (0, 256)
        ]
        outs.append(jnp.concatenate(pieces, axis=1).T)
    out_ref[:, 0:32] = (
        jnp.concatenate([outs[0], outs[1]], axis=1).astype(jnp.bfloat16).reshape(16, 32, 128)
    )
    last = outs[2].reshape(16, 2, 16, HEAD)
    out_ref[:, 32:48] = jnp.concatenate([last[:, 0], last[:, 1]], axis=2).astype(jnp.bfloat16)


def project_kernel(column_ref, row_ref, w_ref, out_ref, joined_ref):
    for pair in range(HALF // 2):
        lanes = slice(128 * pair, 128 * pair + 128)
        for g in range(2):
            even, odd = column_ref[4 * pair + g], column_ref[4 * pair + 2 + g]
            even_last = jnp.concatenate([even[32:, :HEAD], even[32:, HEAD:]], axis=0)
            odd_last = jnp.concatenate([odd[32:, :HEAD], odd[32:, HEAD:]], axis=0)
            joined_ref[3 * g, :, lanes] = jnp.concatenate(
                [even[:32, :HEAD], odd[:32, :HEAD]], axis=1
            )
            joined_ref[3 * g + 1, :, lanes] = jnp.concatenate(
                [even[:32, HEAD:], odd[:32, HEAD:]], axis=1
            )
            joined_ref[3 * g + 2, :, lanes] = jnp.concatenate([even_last, odd_last], axis=1)
        lanes = slice(WIDTH + 128 * pair, WIDTH + 128 * pair + 128)
        for half in range(2):
            blocks = (2 * half, 2 * half + 1)
            even = [row_ref[rg * 8 + 2 * pair].astype(jnp.float32) for rg in blocks]
            odd = [row_ref[rg * 8 + 2 * pair + 1].astype(jnp.float32) for rg in blocks]
            even = jnp.concatenate(even, axis=1)
            odd = jnp.concatenate(odd, axis=1)
            low = low_lanes(even.shape)
            rows = slice(16 * half, 16 * half + 16)
            joined_ref[0:3, rows, lanes] = jnp.where(low, even, swap_halves(odd)).astype(jnp.bfloat16)
            joined_ref[3:6, rows, lanes] = jnp.where(low, swap_halves(even), odd).astype(jnp.bfloat16)
    joined = joined_ref[...].reshape(192, 2 * WIDTH)
    out_ref[...] = (
        lax.dot_general(
            joined, w_ref[...], (((1,), (1,)), ((), ())), preferred_element_type=jnp.float32
        )
        .astype(jnp.bfloat16)
        .reshape(6, 32, 2 * WIDTH)
    )


def kernel_call(kernel, out_shape, name, in_specs, scratch=()):
    vmem = pl.BlockSpec(memory_space=pltpu.VMEM)
    return pl.pallas_call(
        kernel,
        out_shape=jax.ShapeDtypeStruct(out_shape, jnp.bfloat16),
        in_specs=in_specs,
        out_specs=vmem,
        scratch_shapes=list(scratch),
        compiler_params=pltpu.CompilerParams(vmem_limit_bytes=VMEM_LIMIT),
        name=name,
    )


def on_device(query_tokens, key_tokens, value_tokens, merge_sizes, w_out):
    vmem = pl.BlockSpec(memory_space=pltpu.VMEM)
    tokens = [jnp.swapaxes(x, 0, 1) for x in (query_tokens, key_tokens, value_tokens)]
    merges = jnp.transpose(merge_sizes)

    def packed(kernel, which, shape, name):
        return pl.pallas_call(
            kernel,
            out_shape=jax.ShapeDtypeStruct(shape, jnp.bfloat16),
            grid=(1,),
            in_specs=[pl.BlockSpec((6, 32, WIDTH), lambda i: (0, 0, which))] * 3
            + [pl.BlockSpec((6, 32), lambda i: (0, 0))],
            out_specs=pl.BlockSpec(shape, lambda i: (0,) * len(shape)),
            compiler_params=pltpu.CompilerParams(vmem_limit_bytes=VMEM_LIMIT),
            name=name,
        )(*tokens, merges)

    weights = lax.all_gather(jnp.transpose(w_out), "row", axis=0, tiled=True)
    row_packed = packed(pack_rows_kernel, 1, (32, 10, 8, 128), "pack_rows")
    row_moved = lax.all_to_all(row_packed, "col", 0, 0, tiled=True)
    column_packed = packed(pack_columns_kernel, 0, (16, 5, 32, 128), "pack_columns")
    column_moved = lax.all_to_all(column_packed, "row", 0, 0, tiled=True)
    row_out = kernel_call(
        attend_rows_kernel,
        (32, 3, 8, 128),
        "attend_rows",
        [vmem],
        [
            pltpu.VMEM((1536, 128), jnp.float32),
            pltpu.VMEM((768, 128), jnp.float32),
            pltpu.VMEM((256, 128), jnp.float32),
            pltpu.VMEM((768, 128), jnp.float32),
        ],
    )(row_moved)
    row_back = lax.all_to_all(row_out, "col", 0, 0, tiled=True)
    column_out = kernel_call(attend_columns_kernel, (16, 48, 128), "attend_columns", [vmem])(
        column_moved
    )
    column_back = lax.all_to_all(column_out, "row", 0, 0, tiled=True)
    mixed = kernel_call(
        project_kernel,
        (6, 32, 2 * WIDTH),
        "project",
        [vmem] * 3,
        [pltpu.VMEM((6, 32, 2 * WIDTH), jnp.bfloat16)],
    )(column_back, row_back, weights)
    return jnp.swapaxes(mixed, 0, 1)


def solution(mesh):
    return jax.shard_map(
        on_device,
        mesh=mesh,
        in_specs=(
            P("row", "col", None),
            P("row", "col", None),
            P("row", "col", None),
            P("row", "col"),
            P(None, "row"),
        ),
        out_specs=P("row", "col", None),
        check_vma=False,
    )
```

```python
import jax
import jax.numpy as jnp
from jax import lax
from jax.experimental import pallas as pl
from jax.experimental.pallas import tpu as pltpu
from jax.sharding import PartitionSpec as P

HEADS = 16
HEAD = 64
HALF = HEADS // 2
WIDTH = HALF * HEAD
UNIT = 10
W_TILES = 16
SAME_CORE = [list(range(core, 16, 2)) for core in range(2)]
LOG2E = 1.4426950408889634
VMEM_LIMIT = 16 * 1024 * 1024


def swap_halves(tile):
    return pltpu.roll(tile, HEAD, tile.ndim - 1)


def low_lanes(shape):
    return lax.broadcasted_iota(jnp.int32, shape, len(shape) - 1) < HEAD


def bias_lanes(merges, first_token, first_lane, count):
    tokens, rows = merges.shape
    bias = jnp.log(merges.astype(jnp.float32)).astype(jnp.bfloat16).astype(jnp.float32)
    token = lax.broadcasted_iota(jnp.int32, (tokens, 128), 0) - first_token
    lane = lax.broadcasted_iota(jnp.int32, (tokens, 128), 1) - first_lane
    pick = ((token == lane) & (lane >= 0) & (lane < count)).astype(jnp.float32)
    return lax.dot_general(
        bias.astype(jnp.bfloat16),
        pick.astype(jnp.bfloat16),
        (((0,), (0,)), ((), ())),
        preferred_element_type=jnp.float32,
    )


def fetch(sources, targets, sems):
    copies = [
        pltpu.make_async_copy(source, target, sems.at[n])
        for n, (source, target) in enumerate(zip(sources, targets))
    ]
    for copy in copies:
        copy.start()
    for copy in copies:
        copy.wait()


def pack_rows_kernel(q_ref, k_ref, v_ref, m_hbm, out_ref, m_ref, sems):
    fetch([m_hbm], [m_ref], sems)
    bias = bias_lanes(m_ref[...], 0, 0, 6)
    low = low_lanes((6, 32, 128))
    for pair in range(HALF // 2):
        lanes = slice(128 * pair, 128 * pair + 128)
        q = q_ref[:, :, lanes].astype(jnp.float32)
        k = k_ref[:, :, lanes].astype(jnp.float32)
        v = v_ref[:, :, lanes].astype(jnp.float32)
        sq, sk, sv = swap_halves(q), swap_halves(k), swap_halves(v)
        for odd in range(2):
            qk = jnp.where(low, sq, k) if odd else jnp.where(low, q, sk)
            vv = (
                jnp.where(low[:3], sv[:3], v[3:])
                if odd
                else jnp.where(low[:3], v[:3], sv[3:])
            )
            for rg in range(4):
                rows = slice(8 * rg, 8 * rg + 8)
                block = rg * 8 + 2 * pair + odd
                out_ref[block, 0:6] = qk[:, rows].astype(jnp.bfloat16)
                out_ref[block, 6:9] = vv[:, rows].astype(jnp.bfloat16)
                out_ref[block, 9] = bias[rows].astype(jnp.bfloat16)


def place():
    me = lax.axis_index("row")
    return me // 8, (me // 2) % 4, me % 2


def pack_tiles_kernel(q_hbm, k_hbm, v_hbm, m_hbm, w_hbm, send_ref, keep_ref, *refs):
    (*row_refs, m_ref, sems), (y, _, _) = refs, place()
    copies = [(m_hbm, m_ref)]
    for source, target in zip((q_hbm, k_hbm, v_hbm), row_refs):
        copies.append((source.at[:, :, pl.ds(WIDTH, WIDTH)], target))
    for ref, half in ((send_ref, 1 - y), (keep_ref, y)):
        columns = pl.ds(3 * half, 3)
        for pair in range(4):
            for n, source in enumerate((q_hbm, k_hbm, v_hbm)):
                first = UNIT * pair + 3 * n
                lanes = pl.ds(128 * pair, 128)
                copies.append((source.at[columns, :, lanes], ref.at[first : first + 3]))
    for n in range(W_TILES):
        rows, lanes = pl.ds(n % 2 * 32, 32), pl.ds(n // 2 * 128, 128)
        copies.append((w_hbm.at[rows, lanes], send_ref.at[4 * UNIT + n]))
    fetch(*zip(*copies), sems)
    for ref, half in ((send_ref, 1 - y), (keep_ref, y)):
        bias = bias_lanes(m_ref[...], 3 * half, 0, 3).astype(jnp.bfloat16)
        for pair in range(4):
            ref[UNIT * pair + UNIT - 1] = bias


def gather_x_kernel(sent_ref, own_ref, other_ref, *out_refs):
    _, x, _ = place()
    for dx, out_ref in enumerate(out_refs):
        pair = pl.ds((x + dx) % 4 * UNIT, UNIT)
        out_ref[0:UNIT] = own_ref[pair]
        out_ref[UNIT : 2 * UNIT] = other_ref[pair]
        if dx % 2:
            out_ref[2 * UNIT : 2 * UNIT + W_TILES] = sent_ref[4 * UNIT :]
            out_ref[2 * UNIT + W_TILES :] = other_ref[4 * UNIT :]


def early_weights_kernel(sent_ref, other_ref, left_ref, right_ref, early_ref, lack_ref):
    _, x, _ = place()
    early_ref[0:W_TILES] = sent_ref[4 * UNIT :]
    early_ref[W_TILES : 2 * W_TILES] = other_ref[4 * UNIT :]
    early_ref[2 * W_TILES : 4 * W_TILES] = left_ref[2 * UNIT :]
    early_ref[4 * W_TILES :] = right_ref[2 * UNIT :]
    lack_ref[...] = early_ref[pl.ds((2 + 2 * (x % 2)) * W_TILES, 2 * W_TILES)]


def stack_keys_kernel(*refs):
    for dx in range(4):
        for s in range(2):
            first = 14 * dx + 7 * s
            refs[4][first : first + 7] = refs[dx][UNIT * s + 3 : UNIT * s + UNIT]


def assemble_weights_kernel(early_ref, early_other_ref, late_ref, late_other_ref, w_ref):
    y, x, core = place()
    for dc, early, late in ((0, early_ref, late_ref), (1, early_other_ref, late_other_ref)):
        for block in range(8):
            there = (x + (0, 3, 1, 2)[block // 2]) % 4
            part = ((y + block % 2) % 2 * 4 + there) * 2 + (core + dc) % 2
            for n in range(W_TILES):
                rows = pl.ds(pl.multiple_of(part * 64 + n % 2 * 32, 32), 32)
                tile = W_TILES * block + n
                tile = early[tile] if block < 6 else late[tile - 6 * W_TILES]
                w_ref[rows, n // 2 * 128 : n // 2 * 128 + 128] = tile


def attend(q, k, v, bias):
    scores = lax.dot_general(
        k, q, (((1,), (1,)), ((), ())), preferred_element_type=jnp.float32
    )
    scores = scores * (HEAD**-0.5 * LOG2E) + bias * LOG2E
    weights = jnp.exp2(scores - jnp.max(scores, axis=0, keepdims=True))
    totals = jnp.sum(weights, axis=0, keepdims=True)
    summed = lax.dot_general(
        v,
        weights.astype(jnp.bfloat16),
        (((0,), (0,)), ((), ())),
        preferred_element_type=jnp.float32,
    )
    return summed / totals


def attend_rows_kernel(in_ref, after_ref, out_ref, qk_ref, v_ref, b_ref, o_ref):
    for t in range(6):
        qk_ref[t * 256 : t * 256 + 256] = (
            in_ref[:, t].astype(jnp.float32).reshape(256, 128)
        )
    for j in range(3):
        v_ref[j * 256 : j * 256 + 256] = (
            in_ref[:, 6 + j].astype(jnp.float32).reshape(256, 128)
        )
    b_ref[...] = in_ref[:, 9].astype(jnp.float32).reshape(256, 128)
    for r in range(8):
        qk = qk_ref[pl.ds(r, 192, stride=8), :].astype(jnp.bfloat16)
        vv = v_ref[pl.ds(r, 96, stride=8), :].astype(jnp.bfloat16)
        bb = b_ref[pl.ds(r, 32, stride=8), :]
        v = jnp.concatenate([vv[:, :HEAD], vv[:, HEAD:]], axis=0)
        bias = jnp.concatenate([bb[:, t : t + 1] for t in range(6)], axis=0)
        out = attend(qk[:, :HEAD], qk[:, HEAD:], v, bias)
        out = out.T
        o_ref[pl.ds(r, 96, stride=8), :] = jnp.concatenate([out[:96], out[96:]], axis=1)
    for j in range(3):
        out_ref[:, j] = (
            o_ref[j * 256 : j * 256 + 256].reshape(32, 8, 128).astype(jnp.bfloat16)
        )


def attend_columns_kernel(*refs):
    in_refs, other_ref, out_ref = refs[:4], refs[4], refs[5]
    y, x, _ = place()
    sources = [(dx, s) for dx in range(4) for s in range(2)]

    def keys_of(n):
        tiles = [in_refs[dx][UNIT * s + 3 + n] for dx, s in sources]
        tiles += [other_ref[14 * dx + 7 * s + n] for dx, s in sources]
        return jnp.concatenate(tiles, axis=0)

    biases = keys_of(6).astype(jnp.float32) * LOG2E
    low = low_lanes((256, 128))
    for j in range(3):
        q = jnp.concatenate([in_refs[dx][UNIT * s + j] for dx, s in sources], axis=0)
        zero = jnp.zeros_like(q)
        q = jnp.concatenate([jnp.where(low, q, zero), jnp.where(low, zero, q)], axis=0)
        scores = lax.dot_general(
            keys_of(j), q, (((1,), (1,)), ((), ())), preferred_element_type=jnp.float32
        )
        scores = scores * (HEAD**-0.5 * LOG2E) + biases[:, j : j + 1]
        weights = jnp.exp2(scores - jnp.max(scores, axis=0, keepdims=True))
        totals = jnp.sum(weights, axis=0, keepdims=True)
        summed = lax.dot_general(
            keys_of(3 + j),
            weights.astype(jnp.bfloat16),
            (((0,), (0,)), ((), ())),
            preferred_element_type=jnp.float32,
        )
        summed = summed / totals
        out = jnp.concatenate([summed[:HEAD, :256], summed[HEAD:, 256:]], axis=0).T
        out = out.astype(jnp.bfloat16)
        for n, (dx, s) in enumerate(sources):
            out_ref[(y + s) % 2 * 4 + (x - dx + 4) % 4, j] = out[32 * n : 32 * n + 32]


def project_kernel(column_ref, row_ref, w_ref, out_ref, joined_ref):
    for block in range(8):
        lanes = slice(block % 4 * 128, block % 4 * 128 + 128)
        joined_ref[block // 4 * 3 : block // 4 * 3 + 3, :, lanes] = column_ref[block]
    for pair in range(HALF // 2):
        lanes = slice(WIDTH + 128 * pair, WIDTH + 128 * pair + 128)
        for half in range(2):
            blocks = (2 * half, 2 * half + 1)
            even = [row_ref[rg * 8 + 2 * pair].astype(jnp.float32) for rg in blocks]
            odd = [row_ref[rg * 8 + 2 * pair + 1].astype(jnp.float32) for rg in blocks]
            even = jnp.concatenate(even, axis=1)
            odd = jnp.concatenate(odd, axis=1)
            low = low_lanes(even.shape)
            rows = slice(16 * half, 16 * half + 16)
            joined_ref[0:3, rows, lanes] = jnp.where(low, even, swap_halves(odd)).astype(jnp.bfloat16)
            joined_ref[3:6, rows, lanes] = jnp.where(low, swap_halves(even), odd).astype(jnp.bfloat16)
    mixed = lax.dot_general(
        joined_ref[...].reshape(192, 2 * WIDTH),
        w_ref[...],
        (((1,), (1,)), ((), ())),
        preferred_element_type=jnp.float32,
    )
    out_ref[...] = mixed.astype(jnp.bfloat16).reshape(6, 32, 2 * WIDTH)


def call(kernel, out_shapes, name, in_specs, scratch=()):
    vmem = pl.BlockSpec(memory_space=pltpu.VMEM)
    shapes = [jax.ShapeDtypeStruct(shape, jnp.bfloat16) for shape in out_shapes]
    return pl.pallas_call(
        kernel,
        out_shape=shapes,
        in_specs=in_specs,
        out_specs=[vmem] * len(shapes),
        scratch_shapes=list(scratch),
        compiler_params=pltpu.CompilerParams(vmem_limit_bytes=VMEM_LIMIT),
        name=name,
    )


def across_y(array):
    return lax.ppermute(array, "row", [(i, (i + 8) % 16) for i in range(16)])


def across_core(array):
    return lax.ppermute(array, "row", [(i, i // 2 * 2 + (i + 1) % 2) for i in range(16)])


def along_x(array, dx):
    pairs = [(i, i // 8 * 8 + ((i // 2 + dx) % 4) * 2 + i % 2) for i in range(16)]
    return lax.ppermute(array, "row", pairs)


def swap_x(array):
    return lax.ppermute(array, "row", [(i, i ^ 2) for i in range(16)])


def on_device(query_tokens, key_tokens, value_tokens, merge_sizes, w_out):
    vmem = pl.BlockSpec(memory_space=pltpu.VMEM)
    anywhere = pl.BlockSpec(memory_space=pl.ANY)
    hbm = pl.BlockSpec(memory_space=pltpu.HBM)
    tokens = [
        pltpu.with_memory_space_constraint(jnp.swapaxes(x, 0, 1), pltpu.HBM)
        for x in (query_tokens, key_tokens, value_tokens)
    ]
    merges = pltpu.with_memory_space_constraint(jnp.transpose(merge_sizes), pltpu.HBM)
    w_part = pltpu.with_memory_space_constraint(jnp.transpose(w_out), pltpu.HBM)
    sent, own, *row_halves = call(
        pack_tiles_kernel,
        [(4 * UNIT + W_TILES, 32, 128), (4 * UNIT, 32, 128)] + [(6, 32, WIDTH)] * 3,
        "pack_tiles",
        [hbm] * 5,
        [pltpu.VMEM((6, 32), jnp.int32), pltpu.SemaphoreType.DMA((44,))],
    )(*tokens, merges, w_part)
    other = across_y(sent)
    (row_packed,) = call(
        pack_rows_kernel,
        [(32, 10, 8, 128)],
        "pack_rows",
        [vmem] * 3 + [hbm],
        [pltpu.VMEM((6, 32), jnp.int32), pltpu.SemaphoreType.DMA((1,))],
    )(*row_halves, merges)
    row_moved = lax.all_to_all(row_packed, "col", 0, 0, tiled=True)
    by_x = call(
        gather_x_kernel,
        [(2 * UNIT + dx % 2 * 2 * W_TILES, 32, 128) for dx in range(4)],
        "gather_x",
        [vmem] * 3,
    )(sent, own, other)
    by_x = [by_x[0]] + [along_x(by_x[dx], dx) for dx in (1, 2, 3)]
    (keys,) = call(stack_keys_kernel, [(56, 32, 128)], "stack_keys", [vmem] * 4)(*by_x)
    other_keys = across_core(keys)
    early, lack = call(
        early_weights_kernel,
        [(6 * W_TILES, 32, 128), (2 * W_TILES, 32, 128)],
        "early_weights",
        [vmem] * 4,
    )(sent, other, by_x[1], by_x[3])
    late = swap_x(lack)
    weights = [early, across_core(early), late, across_core(late)]
    weights = [pltpu.with_memory_space_constraint(x, pltpu.HBM) for x in weights]
    (column_out,) = call(attend_columns_kernel, [(8, 3, 32, 128)], "attend_columns", [vmem] * 5)(
        *by_x, other_keys
    )
    column_done = column_out
    column_out = lax.all_to_all(
        column_out, "row", 0, 0, tiled=True, axis_index_groups=SAME_CORE
    )
    (row_out,) = call(
        attend_rows_kernel,
        [(32, 3, 8, 128)],
        "attend_rows",
        [vmem, anywhere],
        [
            pltpu.VMEM((1536, 128), jnp.float32),
            pltpu.VMEM((768, 128), jnp.float32),
            pltpu.VMEM((256, 128), jnp.float32),
            pltpu.VMEM((768, 128), jnp.float32),
        ],
    )(row_moved, column_done)
    (weights,) = call(
        assemble_weights_kernel, [(2 * WIDTH, 2 * WIDTH)], "assemble_weights", [vmem] * 4
    )(*weights)
    row_back = lax.all_to_all(row_out, "col", 0, 0, tiled=True)
    (mixed,) = call(
        project_kernel,
        [(6, 32, 2 * WIDTH)],
        "project",
        [vmem] * 3,
        [pltpu.VMEM((6, 32, 2 * WIDTH), jnp.bfloat16)],
    )(column_out, row_back, weights)
    return jnp.swapaxes(mixed, 0, 1)


def solution(mesh):
    return jax.shard_map(
        on_device,
        mesh=mesh,
        in_specs=(
            P("row", "col", None),
            P("row", "col", None),
            P("row", "col", None),
            P("row", "col"),
            P(None, "row"),
        ),
        out_specs=P("row", "col", None),
        check_vma=False,
    )
```

```python
import jax
import jax.numpy as jnp
from jax import lax
from jax.experimental import pallas as pl
from jax.experimental.pallas import tpu as pltpu
from jax.sharding import PartitionSpec as P

HEADS = 16
HEAD = 64
HALF = HEADS // 2
WIDTH = HALF * HEAD
UNIT = 10
W_TILES = 16
SAME_CORE = [list(range(core, 16, 2)) for core in range(2)]
LOG2E = 1.4426950408889634
VMEM_LIMIT = 16 * 1024 * 1024


def swap_halves(tile):
    return pltpu.roll(tile, HEAD, tile.ndim - 1)


def low_lanes(shape):
    return lax.broadcasted_iota(jnp.int32, shape, len(shape) - 1) < HEAD


def bias_lanes(merges, first_token, first_lane, count):
    tokens, rows = merges.shape
    bias = jnp.log(merges.astype(jnp.float32)).astype(jnp.bfloat16).astype(jnp.float32)
    token = lax.broadcasted_iota(jnp.int32, (tokens, 128), 0) - first_token
    lane = lax.broadcasted_iota(jnp.int32, (tokens, 128), 1) - first_lane
    pick = ((token == lane) & (lane >= 0) & (lane < count)).astype(jnp.float32)
    return lax.dot_general(
        bias.astype(jnp.bfloat16),
        pick.astype(jnp.bfloat16),
        (((0,), (0,)), ((), ())),
        preferred_element_type=jnp.float32,
    )


def fetch(sources, targets, sems):
    copies = [
        pltpu.make_async_copy(source, target, sems.at[n])
        for n, (source, target) in enumerate(zip(sources, targets))
    ]
    for copy in copies:
        copy.start()
    for copy in copies:
        copy.wait()


def place():
    me = lax.axis_index("row")
    return me // 8, (me // 2) % 4, me % 2


def pack_rows(q_ref, k_ref, v_ref, m_ref, out_ref):
    bias = bias_lanes(m_ref[...], 0, 0, 6)
    low = low_lanes((6, 32, 128))
    for pair in range(HALF // 2):
        lanes = slice(128 * pair, 128 * pair + 128)
        q = q_ref[:, :, lanes].astype(jnp.float32)
        k = k_ref[:, :, lanes].astype(jnp.float32)
        v = v_ref[:, :, lanes].astype(jnp.float32)
        sq, sk, sv = swap_halves(q), swap_halves(k), swap_halves(v)
        for odd in range(2):
            qk = jnp.where(low, sq, k) if odd else jnp.where(low, q, sk)
            vv = (
                jnp.where(low[:3], sv[:3], v[3:])
                if odd
                else jnp.where(low[:3], v[:3], sv[3:])
            )
            for rg in range(4):
                rows = slice(8 * rg, 8 * rg + 8)
                block = rg * 8 + 2 * pair + odd
                out_ref[block, 0:6] = qk[:, rows].astype(jnp.bfloat16)
                out_ref[block, 6:9] = vv[:, rows].astype(jnp.bfloat16)
                out_ref[block, 9] = bias[rows].astype(jnp.bfloat16)


def pack_kernel(q_hbm, k_hbm, v_hbm, m_hbm, w_hbm, send_ref, keep_ref, out_ref, *refs):
    (*row_refs, m_ref, sems), (y, _, _) = refs, place()
    copies = [(m_hbm, m_ref)]
    for source, target in zip((q_hbm, k_hbm, v_hbm), row_refs):
        copies.append((source.at[:, :, pl.ds(WIDTH, WIDTH)], target))
    for ref, half in ((send_ref, 1 - y), (keep_ref, y)):
        columns = pl.ds(3 * half, 3)
        for pair in range(4):
            for n, source in enumerate((q_hbm, k_hbm, v_hbm)):
                first = UNIT * pair + 3 * n
                lanes = pl.ds(128 * pair, 128)
                copies.append((source.at[columns, :, lanes], ref.at[first : first + 3]))
    for n in range(W_TILES):
        rows, lanes = pl.ds(n % 2 * 32, 32), pl.ds(n // 2 * 128, 128)
        copies.append((w_hbm.at[rows, lanes], send_ref.at[4 * UNIT + n]))
    fetch(*zip(*copies), sems)
    for ref, half in ((send_ref, 1 - y), (keep_ref, y)):
        bias = bias_lanes(m_ref[...], 3 * half, 0, 3).astype(jnp.bfloat16)
        for pair in range(4):
            ref[UNIT * pair + UNIT - 1] = bias
    pack_rows(*row_refs, m_ref, out_ref)


def gather_x_kernel(sent_ref, own_ref, other_ref, *out_refs):
    _, x, _ = place()
    for dx, out_ref in enumerate(out_refs):
        pair = pl.ds((x + dx) % 4 * UNIT, UNIT)
        out_ref[0:UNIT] = own_ref[pair]
        out_ref[UNIT : 2 * UNIT] = other_ref[pair]
        if dx % 2:
            out_ref[2 * UNIT : 2 * UNIT + W_TILES] = sent_ref[4 * UNIT :]
            out_ref[2 * UNIT + W_TILES :] = other_ref[4 * UNIT :]


def early_weights_kernel(sent_ref, other_ref, left_ref, right_ref, early_ref, lack_ref):
    _, x, _ = place()
    early_ref[0:W_TILES] = sent_ref[4 * UNIT :]
    early_ref[W_TILES : 2 * W_TILES] = other_ref[4 * UNIT :]
    early_ref[2 * W_TILES : 4 * W_TILES] = left_ref[2 * UNIT :]
    early_ref[4 * W_TILES :] = right_ref[2 * UNIT :]
    lack_ref[...] = early_ref[pl.ds((2 + 2 * (x % 2)) * W_TILES, 2 * W_TILES)]


def stack_keys_kernel(*refs):
    for dx in range(4):
        for s in range(2):
            first = 14 * dx + 7 * s
            refs[4][first : first + 7] = refs[dx][UNIT * s + 3 : UNIT * s + UNIT]


def assemble_weights_kernel(early_ref, early_other_ref, late_ref, late_other_ref, w_ref):
    y, x, core = place()
    for dc, early, late in ((0, early_ref, late_ref), (1, early_other_ref, late_other_ref)):
        for block in range(8):
            there = (x + (0, 3, 1, 2)[block // 2]) % 4
            part = ((y + block % 2) % 2 * 4 + there) * 2 + (core + dc) % 2
            for n in range(W_TILES):
                rows = pl.ds(pl.multiple_of(part * 64 + n % 2 * 32, 32), 32)
                tile = W_TILES * block + n
                tile = early[tile] if block < 6 else late[tile - 6 * W_TILES]
                w_ref[rows, n // 2 * 128 : n // 2 * 128 + 128] = tile


def attend(q, k, v, bias):
    scores = lax.dot_general(
        k, q, (((1,), (1,)), ((), ())), preferred_element_type=jnp.float32
    )
    scores = scores * (HEAD**-0.5 * LOG2E) + bias * LOG2E
    weights = jnp.exp2(scores - jnp.max(scores, axis=0, keepdims=True))
    totals = jnp.sum(weights, axis=0, keepdims=True)
    summed = lax.dot_general(
        v,
        weights.astype(jnp.bfloat16),
        (((0,), (0,)), ((), ())),
        preferred_element_type=jnp.float32,
    )
    return summed / totals


def attend_rows_kernel(in_ref, after_ref, out_ref, qk_ref, v_ref, b_ref, o_ref):
    for t in range(6):
        qk_ref[t * 256 : t * 256 + 256] = (
            in_ref[:, t].astype(jnp.float32).reshape(256, 128)
        )
    for j in range(3):
        v_ref[j * 256 : j * 256 + 256] = (
            in_ref[:, 6 + j].astype(jnp.float32).reshape(256, 128)
        )
    b_ref[...] = in_ref[:, 9].astype(jnp.float32).reshape(256, 128)
    for r in range(8):
        qk = qk_ref[pl.ds(r, 192, stride=8), :].astype(jnp.bfloat16)
        vv = v_ref[pl.ds(r, 96, stride=8), :].astype(jnp.bfloat16)
        bb = b_ref[pl.ds(r, 32, stride=8), :]
        v = jnp.concatenate([vv[:, :HEAD], vv[:, HEAD:]], axis=0)
        bias = jnp.concatenate([bb[:, t : t + 1] for t in range(6)], axis=0)
        out = attend(qk[:, :HEAD], qk[:, HEAD:], v, bias)
        out = out.T
        o_ref[pl.ds(r, 96, stride=8), :] = jnp.concatenate([out[:96], out[96:]], axis=1)
    for j in range(3):
        out_ref[:, j] = (
            o_ref[j * 256 : j * 256 + 256].reshape(32, 8, 128).astype(jnp.bfloat16)
        )


def attend_columns_kernel(*refs):
    in_refs, other_ref, out_ref = refs[:4], refs[4], refs[5]
    y, x, _ = place()
    sources = [(dx, s) for dx in range(4) for s in range(2)]

    def keys_of(n):
        tiles = [in_refs[dx][UNIT * s + 3 + n] for dx, s in sources]
        tiles += [other_ref[14 * dx + 7 * s + n] for dx, s in sources]
        return jnp.concatenate(tiles, axis=0)

    biases = keys_of(6).astype(jnp.float32) * LOG2E
    low = low_lanes((256, 128))
    for j in range(3):
        q = jnp.concatenate([in_refs[dx][UNIT * s + j] for dx, s in sources], axis=0)
        zero = jnp.zeros_like(q)
        q = jnp.concatenate([jnp.where(low, q, zero), jnp.where(low, zero, q)], axis=0)
        scores = lax.dot_general(
            keys_of(j), q, (((1,), (1,)), ((), ())), preferred_element_type=jnp.float32
        )
        scores = scores * (HEAD**-0.5 * LOG2E) + biases[:, j : j + 1]
        weights = jnp.exp2(scores - jnp.max(scores, axis=0, keepdims=True))
        totals = jnp.sum(weights, axis=0, keepdims=True)
        summed = lax.dot_general(
            keys_of(3 + j),
            weights.astype(jnp.bfloat16),
            (((0,), (0,)), ((), ())),
            preferred_element_type=jnp.float32,
        )
        summed = summed / totals
        out = jnp.concatenate([summed[:HEAD, :256], summed[HEAD:, 256:]], axis=0).T
        out = out.astype(jnp.bfloat16)
        for n, (dx, s) in enumerate(sources):
            out_ref[(y + s) % 2 * 4 + (x - dx + 4) % 4, j] = out[32 * n : 32 * n + 32]


def project_kernel(column_ref, row_ref, w_ref, out_ref, joined_ref):
    for block in range(8):
        lanes = slice(block % 4 * 128, block % 4 * 128 + 128)
        joined_ref[block // 4 * 3 : block // 4 * 3 + 3, :, lanes] = column_ref[block]
    for pair in range(HALF // 2):
        lanes = slice(WIDTH + 128 * pair, WIDTH + 128 * pair + 128)
        for half in range(2):
            blocks = (2 * half, 2 * half + 1)
            even = [row_ref[rg * 8 + 2 * pair].astype(jnp.float32) for rg in blocks]
            odd = [row_ref[rg * 8 + 2 * pair + 1].astype(jnp.float32) for rg in blocks]
            even = jnp.concatenate(even, axis=1)
            odd = jnp.concatenate(odd, axis=1)
            low = low_lanes(even.shape)
            rows = slice(16 * half, 16 * half + 16)
            joined_ref[0:3, rows, lanes] = jnp.where(low, even, swap_halves(odd)).astype(jnp.bfloat16)
            joined_ref[3:6, rows, lanes] = jnp.where(low, swap_halves(even), odd).astype(jnp.bfloat16)
    mixed = lax.dot_general(
        joined_ref[...].reshape(192, 2 * WIDTH),
        w_ref[...],
        (((1,), (1,)), ((), ())),
        preferred_element_type=jnp.float32,
    )
    out_ref[...] = mixed.astype(jnp.bfloat16).reshape(6, 32, 2 * WIDTH)


def call(kernel, out_shapes, name, in_specs, scratch=()):
    vmem = pl.BlockSpec(memory_space=pltpu.VMEM)
    shapes = [jax.ShapeDtypeStruct(shape, jnp.bfloat16) for shape in out_shapes]
    return pl.pallas_call(
        kernel,
        out_shape=shapes,
        in_specs=in_specs,
        out_specs=[vmem] * len(shapes),
        scratch_shapes=list(scratch),
        compiler_params=pltpu.CompilerParams(vmem_limit_bytes=VMEM_LIMIT),
        name=name,
    )


def across_y(array):
    return lax.ppermute(array, "row", [(i, (i + 8) % 16) for i in range(16)])


def across_core(array):
    return lax.ppermute(array, "row", [(i, i // 2 * 2 + (i + 1) % 2) for i in range(16)])


def along_x(array, dx):
    pairs = [(i, i // 8 * 8 + ((i // 2 + dx) % 4) * 2 + i % 2) for i in range(16)]
    return lax.ppermute(array, "row", pairs)


def swap_x(array):
    return lax.ppermute(array, "row", [(i, i ^ 2) for i in range(16)])


def on_device(query_tokens, key_tokens, value_tokens, merge_sizes, w_out):
    vmem = pl.BlockSpec(memory_space=pltpu.VMEM)
    anywhere = pl.BlockSpec(memory_space=pl.ANY)
    hbm = pl.BlockSpec(memory_space=pltpu.HBM)
    tokens = [
        pltpu.with_memory_space_constraint(jnp.swapaxes(x, 0, 1), pltpu.HBM)
        for x in (query_tokens, key_tokens, value_tokens)
    ]
    merges = pltpu.with_memory_space_constraint(jnp.transpose(merge_sizes), pltpu.HBM)
    w_part = pltpu.with_memory_space_constraint(jnp.transpose(w_out), pltpu.HBM)
    sent, own, row_packed = call(
        pack_kernel,
        [(4 * UNIT + W_TILES, 32, 128), (4 * UNIT, 32, 128), (32, 10, 8, 128)],
        "pack",
        [hbm] * 5,
        [pltpu.VMEM((6, 32, WIDTH), jnp.bfloat16)] * 3
        + [pltpu.VMEM((6, 32), jnp.int32), pltpu.SemaphoreType.DMA((44,))],
    )(*tokens, merges, w_part)
    other = across_y(sent)
    row_moved = lax.all_to_all(row_packed, "col", 0, 0, tiled=True)
    by_x = call(
        gather_x_kernel,
        [(2 * UNIT + dx % 2 * 2 * W_TILES, 32, 128) for dx in range(4)],
        "gather_x",
        [vmem] * 3,
    )(sent, own, other)
    by_x = [by_x[0]] + [along_x(by_x[dx], dx) for dx in (1, 2, 3)]
    (keys,) = call(stack_keys_kernel, [(56, 32, 128)], "stack_keys", [vmem] * 4)(*by_x)
    other_keys = across_core(keys)
    early, lack = call(
        early_weights_kernel,
        [(6 * W_TILES, 32, 128), (2 * W_TILES, 32, 128)],
        "early_weights",
        [vmem] * 4,
    )(sent, other, by_x[1], by_x[3])
    late = swap_x(lack)
    weights = [early, across_core(early), late, across_core(late)]
    weights = [pltpu.with_memory_space_constraint(x, pltpu.HBM) for x in weights]
    (column_out,) = call(attend_columns_kernel, [(8, 3, 32, 128)], "attend_columns", [vmem] * 5)(
        *by_x, other_keys
    )
    column_done = column_out
    column_out = lax.all_to_all(
        column_out, "row", 0, 0, tiled=True, axis_index_groups=SAME_CORE
    )
    (row_out,) = call(
        attend_rows_kernel,
        [(32, 3, 8, 128)],
        "attend_rows",
        [vmem, anywhere],
        [
            pltpu.VMEM((1536, 128), jnp.float32),
            pltpu.VMEM((768, 128), jnp.float32),
            pltpu.VMEM((256, 128), jnp.float32),
            pltpu.VMEM((768, 128), jnp.float32),
        ],
    )(row_moved, column_done)
    (weights,) = call(
        assemble_weights_kernel, [(2 * WIDTH, 2 * WIDTH)], "assemble_weights", [vmem] * 4
    )(*weights)
    row_back = lax.all_to_all(row_out, "col", 0, 0, tiled=True)
    (mixed,) = call(
        project_kernel,
        [(6, 32, 2 * WIDTH)],
        "project",
        [vmem] * 3,
        [pltpu.VMEM((6, 32, 2 * WIDTH), jnp.bfloat16)],
    )(column_out, row_back, weights)
    return jnp.swapaxes(mixed, 0, 1)


def solution(mesh):
    return jax.shard_map(
        on_device,
        mesh=mesh,
        in_specs=(
            P("row", "col", None),
            P("row", "col", None),
            P("row", "col", None),
            P("row", "col"),
            P(None, "row"),
        ),
        out_specs=P("row", "col", None),
        check_vma=False,
    )
```

```python
import jax
import jax.numpy as jnp
from jax import lax
from jax.experimental import pallas as pl
from jax.experimental.pallas import tpu as pltpu
from jax.sharding import PartitionSpec as P

HEADS = 16
HEAD = 64
HALF = HEADS // 2
WIDTH = HALF * HEAD
UNIT = 10
X_TILES = 19
CORE_TILES = 13
W_TILES = 16
SAME_CORE = [list(range(core, 16, 2)) for core in range(2)]
LOG2E = 1.4426950408889634
VMEM_LIMIT = 16 * 1024 * 1024


def swap_halves(tile):
    return pltpu.roll(tile, HEAD, tile.ndim - 1)


def low_lanes(shape):
    return lax.broadcasted_iota(jnp.int32, shape, len(shape) - 1) < HEAD


def bias_lanes(merges, first_token, first_lane, count):
    tokens, rows = merges.shape
    bias = jnp.log(merges.astype(jnp.float32)).astype(jnp.bfloat16).astype(jnp.float32)
    token = lax.broadcasted_iota(jnp.int32, (tokens, 128), 0) - first_token
    lane = lax.broadcasted_iota(jnp.int32, (tokens, 128), 1) - first_lane
    pick = ((token == lane) & (lane >= 0) & (lane < count)).astype(jnp.float32)
    return lax.dot_general(
        bias.astype(jnp.bfloat16),
        pick.astype(jnp.bfloat16),
        (((0,), (0,)), ((), ())),
        preferred_element_type=jnp.float32,
    )


def start(copies, sems, first=0):
    started = [pltpu.make_async_copy(*copy, sems.at[first + n]) for n, copy in enumerate(copies)]
    for copy in started:
        copy.start()
    return started


def wait(started):
    for copy in started:
        copy.wait()


def place():
    me = lax.axis_index("row")
    return me // 8, (me // 2) % 4, me % 2


def pack_rows(q_ref, k_ref, v_ref, m_ref, out_ref, out_hbm, sems):
    outgoing = []
    bias = bias_lanes(m_ref[...], 0, 0, 6)
    low = low_lanes((6, 32, 128))
    for pair in range(HALF // 2):
        lanes = slice(128 * pair, 128 * pair + 128)
        q = q_ref[:, :, lanes].astype(jnp.float32)
        k = k_ref[:, :, lanes].astype(jnp.float32)
        v = v_ref[:, :, lanes].astype(jnp.float32)
        sq, sk, sv = swap_halves(q), swap_halves(k), swap_halves(v)
        for odd in range(2):
            qk = jnp.where(low, sq, k) if odd else jnp.where(low, q, sk)
            vv = (
                jnp.where(low[:3], sv[:3], v[3:])
                if odd
                else jnp.where(low[:3], v[:3], sv[3:])
            )
            for rg in range(4):
                rows = slice(8 * rg, 8 * rg + 8)
                h = 2 * pair + odd
                out_ref[rg, h, 0:6] = qk[:, rows].astype(jnp.bfloat16)
                out_ref[rg, h, 6:9] = vv[:, rows].astype(jnp.bfloat16)
                out_ref[rg, h, 9] = bias[rows].astype(jnp.bfloat16)
        heads = pl.ds(2 * pair, 2)
        outgoing += start([(out_ref.at[:, heads], out_hbm.at[:, heads])], sems, pair)
    return outgoing


def pack_kernel(q_hbm, k_hbm, v_hbm, m_hbm, w_hbm, send_ref, keep_ref, out_hbm, *refs):
    (*row_refs, m_ref, sems, out_ref, out_sems), (y, _, _) = refs, place()
    copies = [(m_hbm, m_ref)]
    for source, target in zip((q_hbm, k_hbm, v_hbm), row_refs):
        copies.append((source.at[:, :, pl.ds(WIDTH, WIDTH)], target))
    for ref, half in ((send_ref, 1 - y), (keep_ref, y)):
        columns = pl.ds(3 * half, 3)
        for pair in range(4):
            for n, source in enumerate((q_hbm, k_hbm, v_hbm)):
                first = UNIT * pair + 3 * n
                lanes = pl.ds(128 * pair, 128)
                copies.append((source.at[columns, :, lanes], ref.at[first : first + 3]))
    for n in range(W_TILES):
        rows, lanes = pl.ds(n % 2 * 32, 32), pl.ds(n // 2 * 128, 128)
        copies.append((w_hbm.at[rows, lanes], send_ref.at[4 * UNIT + n]))
    copies = start(copies, sems)
    wait(copies[:4])
    outgoing = pack_rows(*row_refs, m_ref, out_ref, out_hbm, out_sems)
    wait(copies[4:])
    for ref, half in ((send_ref, 1 - y), (keep_ref, y)):
        bias = bias_lanes(m_ref[...], 3 * half, 0, 3).astype(jnp.bfloat16)
        for pair in range(4):
            ref[UNIT * pair + UNIT - 1] = bias
    wait(outgoing)


def shift_lanes(tile, shift):
    return pltpu.roll(tile.astype(jnp.float32), shift, 1)


def gather_x_kernel(sent_ref, own_ref, other_ref, *out_refs):
    _, x, _ = place()
    bias = own_ref[UNIT - 1].astype(jnp.float32) + shift_lanes(other_ref[UNIT - 1], 3)
    for dx, out_ref in enumerate(out_refs):
        pair = pl.ds((x + dx) % 4 * UNIT, 9)
        out_ref[0:9] = own_ref[pair]
        out_ref[9:18] = other_ref[pair]
        out_ref[18] = bias.astype(jnp.bfloat16)
        if dx % 2:
            out_ref[X_TILES : X_TILES + W_TILES] = sent_ref[4 * UNIT :]
            out_ref[X_TILES + W_TILES :] = other_ref[4 * UNIT :]


def early_weights_kernel(sent_ref, other_ref, left_ref, right_ref, early_ref, lack_ref):
    _, x, _ = place()
    early_ref[0:W_TILES] = sent_ref[4 * UNIT :]
    early_ref[W_TILES : 2 * W_TILES] = other_ref[4 * UNIT :]
    early_ref[2 * W_TILES : 4 * W_TILES] = left_ref[X_TILES:]
    early_ref[4 * W_TILES :] = right_ref[X_TILES:]
    lack_ref[...] = early_ref[pl.ds((2 + 2 * (x % 2)) * W_TILES, 2 * W_TILES)]


def stack_keys_kernel(*refs):
    for dx in range(4):
        first = CORE_TILES * dx
        refs[4][first : first + 6] = refs[dx][3:9]
        refs[4][first + 6 : first + 13] = refs[dx][12:19]


def assemble_weights_kernel(early_ref, early_other_ref, late_ref, late_other_ref, w_ref):
    y, x, core = place()
    for dc, early, late in ((0, early_ref, late_ref), (1, early_other_ref, late_other_ref)):
        for block in range(8):
            there = (x + (0, 3, 1, 2)[block // 2]) % 4
            part = ((y + block % 2) % 2 * 4 + there) * 2 + (core + dc) % 2
            for n in range(W_TILES):
                rows = pl.ds(pl.multiple_of(part * 64 + n % 2 * 32, 32), 32)
                tile = W_TILES * block + n
                tile = early[tile] if block < 6 else late[tile - 6 * W_TILES]
                w_ref[rows, n // 2 * 128 : n // 2 * 128 + 128] = tile


def attend(q, k, v, bias):
    scores = lax.dot_general(
        k, q, (((1,), (1,)), ((), ())), preferred_element_type=jnp.float32
    )
    scores = scores * (HEAD**-0.5 * LOG2E) + bias * LOG2E
    weights = jnp.exp2(scores - jnp.max(scores, axis=0, keepdims=True))
    totals = jnp.sum(weights, axis=0, keepdims=True)
    summed = lax.dot_general(
        v,
        weights.astype(jnp.bfloat16),
        (((0,), (0,)), ((), ())),
        preferred_element_type=jnp.float32,
    )
    return summed / totals


def attend_rows_kernel(in_ref, after_ref, out_hbm, qk_ref, v_ref, b_ref, o_ref, out_ref, sems):
    for t in range(6):
        qk_ref[t * 256 : t * 256 + 256] = (
            in_ref[:, t].astype(jnp.float32).reshape(256, 128)
        )
    for j in range(3):
        v_ref[j * 256 : j * 256 + 256] = (
            in_ref[:, 6 + j].astype(jnp.float32).reshape(256, 128)
        )
    b_ref[...] = in_ref[:, 9].astype(jnp.float32).reshape(256, 128)
    for r in range(8):
        qk = qk_ref[pl.ds(r, 192, stride=8), :].astype(jnp.bfloat16)
        vv = v_ref[pl.ds(r, 96, stride=8), :].astype(jnp.bfloat16)
        bb = b_ref[pl.ds(r, 32, stride=8), :]
        v = jnp.concatenate([vv[:, :HEAD], vv[:, HEAD:]], axis=0)
        bias = jnp.concatenate([bb[:, t : t + 1] for t in range(6)], axis=0)
        out = attend(qk[:, :HEAD], qk[:, HEAD:], v, bias)
        out = out.T
        o_ref[pl.ds(r, 96, stride=8), :] = jnp.concatenate([out[:96], out[96:]], axis=1)
    outgoing = []
    for j in range(3):
        out_ref[:, j] = (
            o_ref[j * 256 : j * 256 + 256].reshape(32, 8, 128).astype(jnp.bfloat16)
        )
        outgoing += start([(out_ref.at[:, j], out_hbm.at[:, j])], sems, j)
    wait(outgoing)


def attend_columns_kernel(*refs):
    in_refs, (other_ref, out_hbm, out_ref, sems) = refs[:4], refs[4:]
    outgoing = []
    y, x, _ = place()
    sources = [(dx, s) for dx in range(4) for s in range(2)]

    def keys_of(n):
        tiles = [in_refs[dx][9 * s + 3 + n] for dx, s in sources]
        tiles += [other_ref[CORE_TILES * dx + 6 * s + n] for dx, s in sources]
        return jnp.concatenate(tiles, axis=0)

    biases = [ref[18] for ref in in_refs] + [other_ref[CORE_TILES * dx + 12] for dx in range(4)]
    biases = [shift_lanes(tile, 125 * s % 128) for tile in biases for s in range(2)]
    biases = jnp.concatenate(biases, axis=0) * LOG2E
    low = low_lanes((256, 128))
    for j in range(3):
        q = jnp.concatenate([in_refs[dx][9 * s + j] for dx, s in sources], axis=0)
        zero = jnp.zeros_like(q)
        q = jnp.concatenate([jnp.where(low, q, zero), jnp.where(low, zero, q)], axis=0)
        scores = lax.dot_general(
            keys_of(j), q, (((1,), (1,)), ((), ())), preferred_element_type=jnp.float32
        )
        scores = scores * (HEAD**-0.5 * LOG2E) + biases[:, j : j + 1]
        weights = jnp.exp2(scores - jnp.max(scores, axis=0, keepdims=True))
        totals = jnp.sum(weights, axis=0, keepdims=True)
        summed = lax.dot_general(
            keys_of(3 + j),
            weights.astype(jnp.bfloat16),
            (((0,), (0,)), ((), ())),
            preferred_element_type=jnp.float32,
        )
        summed = summed / totals
        out = jnp.concatenate([summed[:HEAD, :256], summed[HEAD:, 256:]], axis=0).T
        out = out.astype(jnp.bfloat16)
        for n, (dx, s) in enumerate(sources):
            out_ref[(y + s) % 2 * 4 + (x - dx + 4) % 4, j] = out[32 * n : 32 * n + 32]
        outgoing += start([(out_ref.at[:, j], out_hbm.at[:, j])], sems, j)
    wait(outgoing)


def project_kernel(column_ref, row_ref, w_ref, out_hbm, joined_ref, out_ref, sems):
    for block in range(8):
        lanes = slice(block % 4 * 128, block % 4 * 128 + 128)
        joined_ref[block // 4 * 3 : block // 4 * 3 + 3, :, lanes] = column_ref[block]
    for pair in range(HALF // 2):
        lanes = slice(WIDTH + 128 * pair, WIDTH + 128 * pair + 128)
        for half in range(2):
            blocks = (2 * half, 2 * half + 1)
            even = [row_ref[rg * 8 + 2 * pair].astype(jnp.float32) for rg in blocks]
            odd = [row_ref[rg * 8 + 2 * pair + 1].astype(jnp.float32) for rg in blocks]
            even = jnp.concatenate(even, axis=1)
            odd = jnp.concatenate(odd, axis=1)
            low = low_lanes(even.shape)
            rows = slice(16 * half, 16 * half + 16)
            joined_ref[0:3, rows, lanes] = jnp.where(low, even, swap_halves(odd)).astype(jnp.bfloat16)
            joined_ref[3:6, rows, lanes] = jnp.where(low, swap_halves(even), odd).astype(jnp.bfloat16)
    joined = joined_ref[...].reshape(192, 2 * WIDTH)
    outgoing = []
    for n in range(4):
        lanes = pl.ds(256 * n, 256)
        mixed = lax.dot_general(
            joined, w_ref[lanes], (((1,), (1,)), ((), ())), preferred_element_type=jnp.float32
        )
        out_ref[:, :, lanes] = mixed.astype(jnp.bfloat16).reshape(6, 32, 256)
        outgoing += start([(out_ref.at[:, :, lanes], out_hbm.at[:, :, lanes])], sems, n)
    wait(outgoing)


def call(kernel, out_shapes, name, in_specs, scratch=(), out_specs=None):
    vmem = pl.BlockSpec(memory_space=pltpu.VMEM)
    shapes = [jax.ShapeDtypeStruct(shape, jnp.bfloat16) for shape in out_shapes]
    return pl.pallas_call(
        kernel,
        out_shape=shapes,
        in_specs=in_specs,
        out_specs=out_specs or [vmem] * len(shapes),
        scratch_shapes=list(scratch),
        compiler_params=pltpu.CompilerParams(vmem_limit_bytes=VMEM_LIMIT),
        name=name,
    )


def across_y(array):
    return lax.ppermute(array, "row", [(i, (i + 8) % 16) for i in range(16)])


def across_core(array):
    return lax.ppermute(array, "row", [(i, i // 2 * 2 + (i + 1) % 2) for i in range(16)])


def along_x(array, dx):
    pairs = [(i, i // 8 * 8 + ((i // 2 + dx) % 4) * 2 + i % 2) for i in range(16)]
    return lax.ppermute(array, "row", pairs)


def swap_x(array):
    return lax.ppermute(array, "row", [(i, i ^ 2) for i in range(16)])


def on_device(query_tokens, key_tokens, value_tokens, merge_sizes, w_out):
    vmem = pl.BlockSpec(memory_space=pltpu.VMEM)
    anywhere = pl.BlockSpec(memory_space=pl.ANY)
    hbm = pl.BlockSpec(memory_space=pltpu.HBM)
    tokens = [
        pltpu.with_memory_space_constraint(jnp.swapaxes(x, 0, 1), pltpu.HBM)
        for x in (query_tokens, key_tokens, value_tokens)
    ]
    merges = pltpu.with_memory_space_constraint(jnp.transpose(merge_sizes), pltpu.HBM)
    w_part = pltpu.with_memory_space_constraint(jnp.transpose(w_out), pltpu.HBM)
    sent, own, row_packed = call(
        pack_kernel,
        [(4 * UNIT + W_TILES, 32, 128), (4 * UNIT, 32, 128), (4, 8, 10, 8, 128)],
        "pack",
        [hbm] * 5,
        [pltpu.VMEM((6, 32, WIDTH), jnp.bfloat16)] * 3
        + [pltpu.VMEM((6, 32), jnp.int32), pltpu.SemaphoreType.DMA((44,))]
        + [pltpu.VMEM((4, 8, 10, 8, 128), jnp.bfloat16), pltpu.SemaphoreType.DMA((4,))],
        [vmem, vmem, hbm],
    )(*tokens, merges, w_part)
    other = across_y(sent)
    row_moved = lax.all_to_all(row_packed.reshape(32, 10, 8, 128), "col", 0, 0, tiled=True)
    by_x = call(
        gather_x_kernel,
        [(X_TILES + dx % 2 * 2 * W_TILES, 32, 128) for dx in range(4)],
        "gather_x",
        [vmem] * 3,
    )(sent, own, other)
    by_x = [by_x[0]] + [along_x(by_x[dx], dx) for dx in (1, 2, 3)]
    (keys,) = call(stack_keys_kernel, [(4 * CORE_TILES, 32, 128)], "stack_keys", [vmem] * 4)(*by_x)
    other_keys = across_core(keys)
    early, lack = call(
        early_weights_kernel,
        [(6 * W_TILES, 32, 128), (2 * W_TILES, 32, 128)],
        "early_weights",
        [vmem] * 4,
    )(sent, other, by_x[1], by_x[3])
    late = swap_x(lack)
    weights = [early, across_core(early), late, across_core(late)]
    weights = [pltpu.with_memory_space_constraint(x, pltpu.HBM) for x in weights]
    (column_out,) = call(
        attend_columns_kernel,
        [(8, 3, 32, 128)],
        "attend_columns",
        [vmem] * 5,
        [pltpu.VMEM((8, 3, 32, 128), jnp.bfloat16), pltpu.SemaphoreType.DMA((3,))],
        [hbm],
    )(*by_x, other_keys)
    column_done = column_out
    column_out = lax.all_to_all(
        column_out, "row", 0, 0, tiled=True, axis_index_groups=SAME_CORE
    )
    (row_out,) = call(
        attend_rows_kernel,
        [(32, 3, 8, 128)],
        "attend_rows",
        [vmem, anywhere],
        [
            pltpu.VMEM((1536, 128), jnp.float32),
            pltpu.VMEM((768, 128), jnp.float32),
            pltpu.VMEM((256, 128), jnp.float32),
            pltpu.VMEM((768, 128), jnp.float32),
            pltpu.VMEM((32, 3, 8, 128), jnp.bfloat16),
            pltpu.SemaphoreType.DMA((3,)),
        ],
        [hbm],
    )(row_moved, column_done)
    (weights,) = call(
        assemble_weights_kernel, [(2 * WIDTH, 2 * WIDTH)], "assemble_weights", [vmem] * 4
    )(*weights)
    row_back = lax.all_to_all(row_out, "col", 0, 0, tiled=True)
    (mixed,) = call(
        project_kernel,
        [(6, 32, 2 * WIDTH)],
        "project",
        [vmem] * 3,
        [pltpu.VMEM((6, 32, 2 * WIDTH), jnp.bfloat16)] * 2 + [pltpu.SemaphoreType.DMA((4,))],
        [hbm],
    )(column_out, row_back, weights)
    return jnp.swapaxes(mixed, 0, 1)


def solution(mesh):
    return jax.shard_map(
        on_device,
        mesh=mesh,
        in_specs=(
            P("row", "col", None),
            P("row", "col", None),
            P("row", "col", None),
            P("row", "col"),
            P(None, "row"),
        ),
        out_specs=P("row", "col", None),
        check_vma=False,
    )
```

```python
import jax
import jax.numpy as jnp
from jax import lax
from jax.experimental import pallas as pl
from jax.experimental.pallas import tpu as pltpu
from jax.sharding import PartitionSpec as P

HEADS = 16
HEAD = 64
HALF = HEADS // 2
WIDTH = HALF * HEAD
UNIT = 10
X_TILES = 19
CORE_TILES = 13
W_TILES = 16
SAME_CORE = [list(range(core, 16, 2)) for core in range(2)]
LOG2E = 1.4426950408889634
VMEM_LIMIT = 16 * 1024 * 1024


def swap_halves(tile):
    return pltpu.roll(tile, HEAD, tile.ndim - 1)


def low_lanes(shape):
    return lax.broadcasted_iota(jnp.int32, shape, len(shape) - 1) < HEAD


def bias_lanes(merges, first_token, first_lane, count):
    tokens, rows = merges.shape
    bias = jnp.log(merges.astype(jnp.float32)).astype(jnp.bfloat16).astype(jnp.float32)
    token = lax.broadcasted_iota(jnp.int32, (tokens, 128), 0) - first_token
    lane = lax.broadcasted_iota(jnp.int32, (tokens, 128), 1) - first_lane
    pick = ((token == lane) & (lane >= 0) & (lane < count)).astype(jnp.float32)
    return lax.dot_general(
        bias.astype(jnp.bfloat16),
        pick.astype(jnp.bfloat16),
        (((0,), (0,)), ((), ())),
        preferred_element_type=jnp.float32,
    )


def start(copies, sems, first=0):
    started = [pltpu.make_async_copy(*copy, sems.at[first + n]) for n, copy in enumerate(copies)]
    for copy in started:
        copy.start()
    return started


def wait(started):
    for copy in started:
        copy.wait()


def place():
    me = lax.axis_index("row")
    return me // 8, (me // 2) % 4, me % 2


def pack_rows(q_ref, k_ref, v_ref, m_ref, out_ref):
    bias = bias_lanes(m_ref[...], 0, 0, 6)
    low = low_lanes((6, 32, 128))
    for pair in range(HALF // 2):
        lanes = slice(128 * pair, 128 * pair + 128)
        q = q_ref[:, :, lanes].astype(jnp.float32)
        k = k_ref[:, :, lanes].astype(jnp.float32)
        v = v_ref[:, :, lanes].astype(jnp.float32)
        sq, sk, sv = swap_halves(q), swap_halves(k), swap_halves(v)
        for odd in range(2):
            qk = jnp.where(low, sq, k) if odd else jnp.where(low, q, sk)
            vv = (
                jnp.where(low[:3], sv[:3], v[3:])
                if odd
                else jnp.where(low[:3], v[:3], sv[3:])
            )
            for rg in range(4):
                rows = slice(8 * rg, 8 * rg + 8)
                h = 2 * pair + odd
                out_ref[rg, h, 0:6] = qk[:, rows].astype(jnp.bfloat16)
                out_ref[rg, h, 6:9] = vv[:, rows].astype(jnp.bfloat16)
                out_ref[rg, h, 9] = bias[rows].astype(jnp.bfloat16)


def pack_kernel(q_hbm, k_hbm, v_hbm, m_hbm, w_hbm, send_ref, keep_ref, out_ref, *refs):
    (*row_refs, m_ref, sems), (y, _, _) = refs, place()
    copies = [(m_hbm, m_ref)]
    for source, target in zip((q_hbm, k_hbm, v_hbm), row_refs):
        copies.append((source.at[:, :, pl.ds(WIDTH, WIDTH)], target))
    for ref, half in ((send_ref, 1 - y), (keep_ref, y)):
        columns = pl.ds(3 * half, 3)
        for pair in range(4):
            for n, source in enumerate((q_hbm, k_hbm, v_hbm)):
                first = UNIT * pair + 3 * n
                lanes = pl.ds(128 * pair, 128)
                copies.append((source.at[columns, :, lanes], ref.at[first : first + 3]))
    for n in range(W_TILES):
        rows, lanes = pl.ds(n % 2 * 32, 32), pl.ds(n // 2 * 128, 128)
        copies.append((w_hbm.at[rows, lanes], send_ref.at[4 * UNIT + n]))
    copies = start(copies, sems)
    wait(copies[:4])
    pack_rows(*row_refs, m_ref, out_ref)
    wait(copies[4:])
    for ref, half in ((send_ref, 1 - y), (keep_ref, y)):
        bias = bias_lanes(m_ref[...], 3 * half, 0, 3).astype(jnp.bfloat16)
        for pair in range(4):
            ref[UNIT * pair + UNIT - 1] = bias


def shift_lanes(tile, shift):
    return pltpu.roll(tile.astype(jnp.float32), shift, 1)


def gather_x_kernel(sent_ref, own_ref, other_ref, *out_refs):
    _, x, _ = place()
    bias = own_ref[UNIT - 1].astype(jnp.float32) + shift_lanes(other_ref[UNIT - 1], 3)
    for dx, out_ref in enumerate(out_refs):
        pair = pl.ds((x + dx) % 4 * UNIT, 9)
        out_ref[0:9] = own_ref[pair]
        out_ref[9:18] = other_ref[pair]
        out_ref[18] = bias.astype(jnp.bfloat16)
        if dx % 2:
            out_ref[X_TILES : X_TILES + W_TILES] = sent_ref[4 * UNIT :]
            out_ref[X_TILES + W_TILES :] = other_ref[4 * UNIT :]


def early_weights_kernel(sent_ref, other_ref, left_ref, right_ref, early_ref, lack_ref):
    _, x, _ = place()
    early_ref[0:W_TILES] = sent_ref[4 * UNIT :]
    early_ref[W_TILES : 2 * W_TILES] = other_ref[4 * UNIT :]
    early_ref[2 * W_TILES : 4 * W_TILES] = left_ref[X_TILES:]
    early_ref[4 * W_TILES :] = right_ref[X_TILES:]
    lack_ref[...] = early_ref[pl.ds((2 + 2 * (x % 2)) * W_TILES, 2 * W_TILES)]


def stack_keys_kernel(*refs):
    for dx in range(4):
        first = CORE_TILES * dx
        refs[4][first : first + 6] = refs[dx][3:9]
        refs[4][first + 6 : first + 13] = refs[dx][12:19]


def assemble_weights_kernel(early_ref, early_other_ref, late_ref, late_other_ref, w_ref):
    y, x, core = place()
    for dc, early, late in ((0, early_ref, late_ref), (1, early_other_ref, late_other_ref)):
        for block in range(8):
            there = (x + (0, 3, 1, 2)[block // 2]) % 4
            part = ((y + block % 2) % 2 * 4 + there) * 2 + (core + dc) % 2
            for n in range(W_TILES):
                rows = pl.ds(pl.multiple_of(part * 64 + n % 2 * 32, 32), 32)
                tile = W_TILES * block + n
                tile = early[tile] if block < 6 else late[tile - 6 * W_TILES]
                w_ref[rows, n // 2 * 128 : n // 2 * 128 + 128] = tile


def attend(q, k, v, bias):
    scores = lax.dot_general(
        k, q, (((1,), (1,)), ((), ())), preferred_element_type=jnp.float32
    )
    scores = scores * (HEAD**-0.5 * LOG2E) + bias * LOG2E
    weights = jnp.exp2(scores - jnp.max(scores, axis=0, keepdims=True))
    totals = jnp.sum(weights, axis=0, keepdims=True)
    summed = lax.dot_general(
        v,
        weights.astype(jnp.bfloat16),
        (((0,), (0,)), ((), ())),
        preferred_element_type=jnp.float32,
    )
    return summed / totals


def attend_rows_kernel(in_ref, after_ref, out_ref, qk_ref, v_ref, b_ref, o_ref):
    for t in range(6):
        qk_ref[t * 256 : t * 256 + 256] = (
            in_ref[:, t].astype(jnp.float32).reshape(256, 128)
        )
    for j in range(3):
        v_ref[j * 256 : j * 256 + 256] = (
            in_ref[:, 6 + j].astype(jnp.float32).reshape(256, 128)
        )
    b_ref[...] = in_ref[:, 9].astype(jnp.float32).reshape(256, 128)
    for r in range(8):
        qk = qk_ref[pl.ds(r, 192, stride=8), :].astype(jnp.bfloat16)
        vv = v_ref[pl.ds(r, 96, stride=8), :].astype(jnp.bfloat16)
        bb = b_ref[pl.ds(r, 32, stride=8), :]
        v = jnp.concatenate([vv[:, :HEAD], vv[:, HEAD:]], axis=0)
        bias = jnp.concatenate([bb[:, t : t + 1] for t in range(6)], axis=0)
        out = attend(qk[:, :HEAD], qk[:, HEAD:], v, bias)
        out = out.T
        o_ref[pl.ds(r, 96, stride=8), :] = jnp.concatenate([out[:96], out[96:]], axis=1)
    for j in range(3):
        out_ref[:, j] = (
            o_ref[j * 256 : j * 256 + 256].reshape(32, 8, 128).astype(jnp.bfloat16)
        )


def attend_columns_kernel(*refs):
    in_refs, (other_ref, out_hbm, out_ref, sems) = refs[:4], refs[4:]
    outgoing = []
    y, x, _ = place()
    sources = [(dx, s) for dx in range(4) for s in range(2)]

    def keys_of(n):
        tiles = [in_refs[dx][9 * s + 3 + n] for dx, s in sources]
        tiles += [other_ref[CORE_TILES * dx + 6 * s + n] for dx, s in sources]
        return jnp.concatenate(tiles, axis=0)

    biases = [ref[18] for ref in in_refs] + [other_ref[CORE_TILES * dx + 12] for dx in range(4)]
    biases = [shift_lanes(tile, 125 * s % 128) for tile in biases for s in range(2)]
    biases = jnp.concatenate(biases, axis=0) * LOG2E
    low = low_lanes((256, 128))
    for j in range(3):
        q = jnp.concatenate([in_refs[dx][9 * s + j] for dx, s in sources], axis=0)
        zero = jnp.zeros_like(q)
        q = jnp.concatenate([jnp.where(low, q, zero), jnp.where(low, zero, q)], axis=0)
        scores = lax.dot_general(
            keys_of(j), q, (((1,), (1,)), ((), ())), preferred_element_type=jnp.float32
        )
        scores = scores * (HEAD**-0.5 * LOG2E) + biases[:, j : j + 1]
        weights = jnp.exp2(scores - jnp.max(scores, axis=0, keepdims=True))
        totals = jnp.sum(weights, axis=0, keepdims=True)
        summed = lax.dot_general(
            keys_of(3 + j),
            weights.astype(jnp.bfloat16),
            (((0,), (0,)), ((), ())),
            preferred_element_type=jnp.float32,
        )
        summed = summed / totals
        out = jnp.concatenate([summed[:HEAD, :256], summed[HEAD:, 256:]], axis=0).T
        out = out.astype(jnp.bfloat16)
        for n, (dx, s) in enumerate(sources):
            out_ref[(y + s) % 2 * 4 + (x - dx + 4) % 4, j] = out[32 * n : 32 * n + 32]
        outgoing += start([(out_ref.at[:, j], out_hbm.at[:, j])], sems, j)
    wait(outgoing)


def project_kernel(column_ref, row_ref, w_ref, out_hbm, joined_ref, out_ref, sems):
    for block in range(8):
        lanes = slice(block % 4 * 128, block % 4 * 128 + 128)
        joined_ref[block // 4 * 3 : block // 4 * 3 + 3, :, lanes] = column_ref[block]
    for pair in range(HALF // 2):
        lanes = slice(WIDTH + 128 * pair, WIDTH + 128 * pair + 128)
        for half in range(2):
            blocks = (2 * half, 2 * half + 1)
            even = [row_ref[rg * 8 + 2 * pair].astype(jnp.float32) for rg in blocks]
            odd = [row_ref[rg * 8 + 2 * pair + 1].astype(jnp.float32) for rg in blocks]
            even = jnp.concatenate(even, axis=1)
            odd = jnp.concatenate(odd, axis=1)
            low = low_lanes(even.shape)
            rows = slice(16 * half, 16 * half + 16)
            joined_ref[0:3, rows, lanes] = jnp.where(low, even, swap_halves(odd)).astype(jnp.bfloat16)
            joined_ref[3:6, rows, lanes] = jnp.where(low, swap_halves(even), odd).astype(jnp.bfloat16)
    joined = joined_ref[...].reshape(192, 2 * WIDTH)
    outgoing = []
    for n in range(4):
        lanes = pl.ds(256 * n, 256)
        mixed = lax.dot_general(
            joined, w_ref[lanes], (((1,), (1,)), ((), ())), preferred_element_type=jnp.float32
        )
        out_ref[:, :, lanes] = mixed.astype(jnp.bfloat16).reshape(6, 32, 256)
        outgoing += start([(out_ref.at[:, :, lanes], out_hbm.at[:, :, lanes])], sems, n)
    wait(outgoing)


def call(kernel, out_shapes, name, in_specs, scratch=(), out_specs=None):
    vmem = pl.BlockSpec(memory_space=pltpu.VMEM)
    shapes = [jax.ShapeDtypeStruct(shape, jnp.bfloat16) for shape in out_shapes]
    return pl.pallas_call(
        kernel,
        out_shape=shapes,
        in_specs=in_specs,
        out_specs=out_specs or [vmem] * len(shapes),
        scratch_shapes=list(scratch),
        compiler_params=pltpu.CompilerParams(vmem_limit_bytes=VMEM_LIMIT),
        name=name,
    )


def across_y(array):
    return lax.ppermute(array, "row", [(i, (i + 8) % 16) for i in range(16)])


def across_core(array):
    return lax.ppermute(array, "row", [(i, i // 2 * 2 + (i + 1) % 2) for i in range(16)])


def along_x(array, dx):
    pairs = [(i, i // 8 * 8 + ((i // 2 + dx) % 4) * 2 + i % 2) for i in range(16)]
    return lax.ppermute(array, "row", pairs)


def swap_x(array):
    return lax.ppermute(array, "row", [(i, i ^ 2) for i in range(16)])


def on_device(query_tokens, key_tokens, value_tokens, merge_sizes, w_out):
    vmem = pl.BlockSpec(memory_space=pltpu.VMEM)
    anywhere = pl.BlockSpec(memory_space=pl.ANY)
    hbm = pl.BlockSpec(memory_space=pltpu.HBM)
    tokens = [
        pltpu.with_memory_space_constraint(jnp.swapaxes(x, 0, 1), pltpu.HBM)
        for x in (query_tokens, key_tokens, value_tokens)
    ]
    merges = pltpu.with_memory_space_constraint(jnp.transpose(merge_sizes), pltpu.HBM)
    w_part = pltpu.with_memory_space_constraint(jnp.transpose(w_out), pltpu.HBM)
    sent, own, row_packed = call(
        pack_kernel,
        [(4 * UNIT + W_TILES, 32, 128), (4 * UNIT, 32, 128), (4, 8, 10, 8, 128)],
        "pack",
        [hbm] * 5,
        [pltpu.VMEM((6, 32, WIDTH), jnp.bfloat16)] * 3
        + [pltpu.VMEM((6, 32), jnp.int32), pltpu.SemaphoreType.DMA((44,))],
    )(*tokens, merges, w_part)
    other = across_y(sent)
    row_moved = lax.all_to_all(row_packed.reshape(32, 10, 8, 128), "col", 0, 0, tiled=True)
    by_x = call(
        gather_x_kernel,
        [(X_TILES + dx % 2 * 2 * W_TILES, 32, 128) for dx in range(4)],
        "gather_x",
        [vmem] * 3,
    )(sent, own, other)
    by_x = [by_x[0]] + [along_x(by_x[dx], dx) for dx in (1, 2, 3)]
    (keys,) = call(stack_keys_kernel, [(4 * CORE_TILES, 32, 128)], "stack_keys", [vmem] * 4)(*by_x)
    other_keys = across_core(keys)
    early, lack = call(
        early_weights_kernel,
        [(6 * W_TILES, 32, 128), (2 * W_TILES, 32, 128)],
        "early_weights",
        [vmem] * 4,
    )(sent, other, by_x[1], by_x[3])
    late = swap_x(lack)
    weights = [early, across_core(early), late, across_core(late)]
    weights = [pltpu.with_memory_space_constraint(x, pltpu.HBM) for x in weights]
    (column_out,) = call(
        attend_columns_kernel,
        [(8, 3, 32, 128)],
        "attend_columns",
        [vmem] * 5,
        [pltpu.VMEM((8, 3, 32, 128), jnp.bfloat16), pltpu.SemaphoreType.DMA((3,))],
        [hbm],
    )(*by_x, other_keys)
    column_done = column_out
    column_out = lax.all_to_all(
        column_out, "row", 0, 0, tiled=True, axis_index_groups=SAME_CORE
    )
    (row_out,) = call(
        attend_rows_kernel,
        [(32, 3, 8, 128)],
        "attend_rows",
        [vmem, anywhere],
        [
            pltpu.VMEM((1536, 128), jnp.float32),
            pltpu.VMEM((768, 128), jnp.float32),
            pltpu.VMEM((256, 128), jnp.float32),
            pltpu.VMEM((768, 128), jnp.float32),
        ],
    )(row_moved, column_done)
    (weights,) = call(
        assemble_weights_kernel, [(2 * WIDTH, 2 * WIDTH)], "assemble_weights", [vmem] * 4
    )(*weights)
    row_back = lax.all_to_all(row_out, "col", 0, 0, tiled=True)
    (mixed,) = call(
        project_kernel,
        [(6, 32, 2 * WIDTH)],
        "project",
        [vmem] * 3,
        [pltpu.VMEM((6, 32, 2 * WIDTH), jnp.bfloat16)] * 2 + [pltpu.SemaphoreType.DMA((4,))],
        [hbm],
    )(column_out, row_back, weights)
    return jnp.swapaxes(mixed, 0, 1)


def solution(mesh):
    return jax.shard_map(
        on_device,
        mesh=mesh,
        in_specs=(
            P("row", "col", None),
            P("row", "col", None),
            P("row", "col", None),
            P("row", "col"),
            P(None, "row"),
        ),
        out_specs=P("row", "col", None),
        check_vma=False,
    )
```
